128 devices in a mesh: river: 8 (over y, core), coast: 16 (over z, x).
Axes of the slice: x: 4, y: 4, z: 4, core: 2. Of those that a mesh axis runs over, the one named last changes fastest.
Arguments:
- reach_depth: float32 [8192, 128], P(('river', 'coast')), may hold values from 0.02 to 4
- reach_flow: float32 [8192, 128], P(('river', 'coast')), may hold values from -3 to 3
- reach_bed: float32 [8192, 128], P(('river', 'coast')), may hold values from 0 to 1
- reach_width: float32 [8192, 128], P(('river', 'coast')), may hold values from 200 to 800
- reach_length: float32 [8192, 128], P(('river', 'coast')), may hold values from 4000 to 12000
- runoff: float32 [8192, 128], P(('river', 'coast')), may hold values from 1 to 100
- flows_into: int32 [8192, 128], P(('river', 'coast')), may hold values from 1 to 128, as said below
- mouth_prev: float32 [8192, 32], P(('river', 'coast')), may hold values from -1.5 to 1.5
- mouth_tile: int32 [8192, 32, 1], P(('river', 'coast')), may hold values from 0 to 127; in each aligned block of 2048 rows (0 to 2047, 2048 to 4095, ..., all dimensions but the last counted through in order) at most 32 rows name the same one
- mouth_cell: int32 [8192, 32], P(('river', 'coast')), may hold values from 0 to 4095
- sea_level: float32 [256, 2048], P('river', 'coast'), may hold values from -1.2 to 1.2
- sea_bed: float32 [256, 2048], P('river', 'coast'), may hold values from -4 to 0.5
- wet_mask: int32 [256, 2048], P('river', 'coast'), may hold values 0 or 1
- flux_east: float32 [256, 2048], P('river', 'coast'), may hold values from -3 to 3
- flux_north: float32 [256, 2048], P('river', 'coast'), may hold values from -3 to 3
Outputs:
- depth_after: float32 [8192, 128], P(('river', 'coast'))
- level_after: float32 [256, 2048], P('river', 'coast')
- mouth_level: float32 [8192, 384], P(('river', 'coast'))
The draws below stay inside these ranges and needn't reach their ends.
Inputs may be any that keep to these rules, and one draw needn't show every extreme that they name: `flows_into`: in every block the last 32 reaches have the value 128 (they flow to the sea); every other reach i names a reach of the same block with index i + 1 to i + 16. `mouth_tile`: among the mouths of one device (the rows of one device, in order), no tile is named more than 32 times, a bound that some block reaches; every tile is named by some mouth.
All inputs are finite; a program needn't handle non-finite values. No bound on the sum of `wet_mask` on one device may be relied on, other than what follows from the above.
Results may differ from the reference program's by a relative error of at most 0.0002.
Values sent between devices are 32-bit elements; how exact they have to be, the bound alone decides.
A program may use at most 64 MiB of HBM per device.

```python
import math
import jax
import jax.numpy as jnp
import numpy as np

RB = 128
MPB = 32
STEPS = 12
BLK_DEV = 64
TX = 32
TY = 128
CAP = 32
NBLK = 8192
OX = 256
OY = 2048
N_COAST = 16
DEVICES = 128


def draw_flows_into(key, part):
    position = jnp.broadcast_to(jnp.arange(RB, dtype=jnp.int32)[None, :], (NBLK, RB))
    lowest = jnp.minimum(position + 1, RB - 1)
    highest = jnp.maximum(jnp.minimum(position + 17, RB), lowest + 1)
    picked = jax.random.randint(key, (NBLK, RB), lowest, highest, dtype=jnp.int32)
    return jnp.where(position >= RB - MPB, RB, picked).astype(jnp.int32)


def set_ends(values, key, smallest, high):
    index_at = [jax.random.randint(jax.random.fold_in(key, axis), (), 0, length) for axis, length in enumerate(values.shape)]
    widest = values.shape.index(max(values.shape))
    neighbour = index_at[:widest] + [(index_at[widest] + 1) % values.shape[widest]] + index_at[widest + 1:]
    return values.at[tuple(index_at)].set(smallest).at[tuple(neighbour)].set(high)


def block_scale(own_key, shape, pieces, low, largest):
    def one(dim, shards_of):
        draws = jax.random.uniform(jax.random.fold_in(jax.random.fold_in(own_key, 6), dim), (shards_of,), jnp.float32, low / len(pieces), largest / len(pieces))
        return jnp.repeat(jnp.exp(draws), shape[dim] // shards_of).reshape((-1,) + (1,) * (len(shape) - dim - 1))

    level = one(*pieces[0])
    for cut in pieces[1:]:
        level = level * one(*cut)
    return level


def deal_out(own_key, own, number, rows, amount, top, bound, skew):
    sequence = jax.random.permutation(own_key, amount)
    packed, common = portions_of(amount, rows * top, bound, skew, True), portions_of(amount, rows * top, bound, skew, False)
    places = jnp.arange(amount)

    def named(sizes, turn):
        used = int((sizes > 0).sum())
        fixed = max(1, used // 4)
        passed = fixed + (places - fixed + turn * (used - fixed)) % max(1, amount - fixed)
        return jnp.zeros((amount,), jnp.int32).at[sequence[jnp.where(places < fixed, places, passed)]].set(jnp.asarray(sizes, jnp.int32))

    sizes = jnp.where(number % 4 == 0, named(packed, number // 4), named(common, number - number // 4 - 1))
    mixed = jax.random.permutation(jax.random.fold_in(own, 3), amount)
    donor, receiver = mixed[0:amount // 2 * 2:2], mixed[1:amount // 2 * 2:2]
    margin = jnp.minimum(sizes[donor] - 1, bound - sizes[receiver]) // 2
    margin = jnp.where((donor == sequence[0]) | (receiver == sequence[0]) | (sizes[receiver] == 0), 0, jnp.maximum(margin, 0))
    passed = jax.random.randint(jax.random.fold_in(own, 4), (amount // 2,), 0, 1 << 20) % (margin + 1)
    sizes = sizes.at[donor].add(-passed).at[receiver].add(passed)
    labels = jnp.searchsorted(jnp.cumsum(sizes), jnp.arange(rows * top), side="right").astype(jnp.int32)
    listing = labels.reshape(top, rows).T
    listing = listing[jax.random.permutation(jax.random.fold_in(own, 1), rows)]
    turn = jax.random.randint(jax.random.fold_in(own, 2), (rows, 1), 0, top)
    return jnp.take_along_axis(listing, (jnp.arange(top)[None, :] + turn) % top, axis=1)


def portions_of(amount, total, bound, lean, full):
    loads = [(1 << 20) // math.isqrt(grade ** lean) + 1 for grade in range(1, amount + 1)]
    largest = bound if full else min(bound, max(-(-total // amount), total * loads[0] // sum(loads)))
    least = 1 if total - largest >= amount - 1 else 0
    given, spare = [largest] + [least] * (amount - 1), total - largest - least * (amount - 1)
    while spare > 0:
        movable = [i for i in range(1, amount) if given[i] < largest] or [i for i in range(1, amount) if given[i] < bound]
        mass, budget = sum([loads[i] for i in movable]), spare
        for i in movable:
            more = min(bound - given[i], max(1, budget * loads[i] // mass), spare)
            given[i] = given[i] + more
            spare = spare - more
    return np.array(given)


def bell_draw(key, dims, scale, limit, cuts=(), kind=jnp.bfloat16):
    factor_of = block_scale(key, dims, cuts, -0.22, 0.18) if cuts else 1.0
    result = jax.random.normal(key, dims, jnp.float32) * scale * factor_of
    return jnp.minimum(jnp.maximum(result, -limit), limit).astype(kind)


def setup_inputs(seed: int = 0) -> dict:
    arg_keys = jax.random.split(jax.random.key(seed), 16)
    reach_depth = jnp.clip(jnp.exp(math.log(4.0) - 5.2983174 * jax.random.uniform(arg_keys[0], (NBLK, RB), jnp.float32) ** block_scale(arg_keys[0], (NBLK, RB), ((0, 128),), -0.2, 0.2)), 0.02, 4.0)
    reach_flow = bell_draw(arg_keys[1], (NBLK, RB), 0.5, 3.0, ((0, 128),), jnp.float32)
    reach_bed = jnp.clip(1.0 * jax.random.uniform(arg_keys[2], (NBLK, RB), jnp.float32) ** block_scale(arg_keys[2], (NBLK, RB), ((0, 128),), -0.2, 0.2), 0.0, 1.0)
    reach_width = jnp.clip(jnp.exp(math.log(800.0) - 1.3862944 * jax.random.uniform(arg_keys[3], (NBLK, RB), jnp.float32) ** block_scale(arg_keys[3], (NBLK, RB), ((0, 128),), -0.2, 0.2)), 200.0, 800.0)
    reach_length = jnp.clip(jnp.exp(math.log(12000.0) - 1.0986123 * jax.random.uniform(arg_keys[4], (NBLK, RB), jnp.float32) ** block_scale(arg_keys[4], (NBLK, RB), ((0, 128),), -0.2, 0.2)), 4000.0, 12000.0)
    runoff = jnp.clip(jnp.exp(math.log(100.0) - 4.6051702 * jax.random.uniform(arg_keys[5], (NBLK, RB), jnp.float32) ** block_scale(arg_keys[5], (NBLK, RB), ((0, 128),), -0.2, 0.2)), 1.0, 100.0)
    flows_into = draw_flows_into(jax.random.fold_in(arg_keys[15], 71), 0)
    mouth_prev = bell_draw(arg_keys[7], (NBLK, MPB), 0.4, 1.5, ((0, 128),), jnp.float32)
    mouth_tile_keys = jax.random.split(jax.random.fold_in(arg_keys[8], 1), NBLK * MPB // (BLK_DEV * MPB))
    mouth_tile_turns = jax.random.permutation(jax.random.fold_in(arg_keys[8], 3), NBLK * MPB // (BLK_DEV * MPB))
    mouth_tile = jax.vmap(lambda own, number: deal_out(jax.random.fold_in(arg_keys[8], 2), own, number, BLK_DEV * MPB, DEVICES, 1, CAP, 2))(mouth_tile_keys, mouth_tile_turns).reshape((NBLK, MPB, 1))
    mouth_cell = set_ends(jax.random.randint(arg_keys[9], (NBLK, MPB), 0, TX * TY), jax.random.fold_in(arg_keys[9], 1), 0, (TX * TY) - 1).astype(jnp.int32)
    sea_level = bell_draw(arg_keys[10], (OX, OY), 0.3, 1.2, ((0, 8), (1, 16)), jnp.float32)
    sea_bed = jnp.clip(-4.0 + 4.5 * jax.random.uniform(arg_keys[11], (OX, OY), jnp.float32) ** block_scale(arg_keys[11], (OX, OY), ((0, 8), (1, 16)), -0.2, 0.2), -4.0, 0.5)
    wet_mask = set_ends((jax.random.randint(arg_keys[12], (OX, OY), 0, 8) < 7).astype(jnp.int32), jax.random.fold_in(arg_keys[12], 1), 0, 1)
    flux_east = bell_draw(arg_keys[13], (OX, OY), 0.5, 3.0, ((0, 8), (1, 16)), jnp.float32)
    flux_north = bell_draw(arg_keys[14], (OX, OY), 0.5, 3.0, ((0, 8), (1, 16)), jnp.float32)
    return dict(reach_depth=reach_depth, reach_flow=reach_flow, reach_bed=reach_bed, reach_width=reach_width, reach_length=reach_length, runoff=runoff, flows_into=flows_into, mouth_prev=mouth_prev, mouth_tile=mouth_tile, mouth_cell=mouth_cell, sea_level=sea_level, sea_bed=sea_bed, wet_mask=wet_mask, flux_east=flux_east, flux_north=flux_north)


gravity = 9.81
step_seconds = 300.0
cell_metres = 3000.0
river_manning = 0.035
ocean_manning = 0.025
depth_floor = 0.05


def inertial(unit_flow, upper_level, lower_level, bed_upper, bed_lower, distance, manning):
    face_depth = jnp.maximum(upper_level, lower_level) - jnp.maximum(bed_upper, bed_lower)
    driving = gravity * step_seconds * jnp.maximum(face_depth, 0.0) * (upper_level - lower_level) / distance
    friction = gravity * step_seconds * manning * manning * jnp.abs(unit_flow) / jnp.power(jnp.maximum(face_depth, depth_floor), 7.0 / 3.0)
    return (unit_flow + driving) / (1.0 + friction)


def river_step(water_depth, unit_flow, reach_bed, reach_width, reach_length, runoff, flows_into, mouth_prev):
    inland = RB - MPB
    surface = reach_bed + water_depth
    down_index = flows_into[:, :inland].astype(jnp.int32)
    below = jnp.concatenate([jnp.take_along_axis(surface, down_index, axis=1), mouth_prev], axis=1)
    bed_below = jnp.concatenate([jnp.take_along_axis(reach_bed, down_index, axis=1), reach_bed[:, inland:]], axis=1)
    unit_flow = inertial(unit_flow, surface, below, reach_bed, bed_below, reach_length, river_manning)
    discharge = unit_flow * reach_width
    row_index = jnp.arange(water_depth.shape[0], dtype=jnp.int32)[:, None]
    inflow = jnp.zeros_like(water_depth).at[row_index, down_index].add(discharge[:, :inland])
    water_depth = water_depth + step_seconds * (inflow + runoff - discharge) / (reach_width * reach_length)
    return water_depth, unit_flow, discharge[:, inland:]


def reference(reach_depth, reach_flow, reach_bed, reach_width, reach_length, runoff, flows_into, mouth_prev, mouth_tile, mouth_cell, sea_level, sea_bed, wet_mask, flux_east, flux_north):
    tile_index = mouth_tile[:, :, 0]
    grid_row = (tile_index // N_COAST) * TX + mouth_cell // TY
    grid_col = (tile_index % N_COAST) * TY + mouth_cell % TY
    target = (grid_row * OY + grid_col).reshape(-1).astype(jnp.int32)
    water_level = jnp.where(wet_mask == 1, jnp.maximum(sea_level, sea_bed), sea_bed)
    bed_padded = jnp.pad(sea_bed, 1)
    east_faces = jnp.concatenate([jnp.zeros((1, OY), jnp.float32), flux_east], axis=0)
    north_faces = jnp.concatenate([jnp.zeros((OX, 1), jnp.float32), flux_north], axis=1)
    water_depth, unit_flow = reach_depth, reach_flow
    sampled = []
    for substep in range(STEPS):
        water_depth, unit_flow, mouth_flow = river_step(water_depth, unit_flow, reach_bed, reach_width, reach_length, runoff, flows_into, mouth_prev)
        source = jnp.zeros((OX * OY,), jnp.float32).at[target].add(mouth_flow.reshape(-1)).reshape(OX, OY)
        padded = jnp.pad(water_level, 1)
        east_faces = inertial(east_faces, padded[:-1, 1:-1], padded[1:, 1:-1], bed_padded[:-1, 1:-1], bed_padded[1:, 1:-1], cell_metres, ocean_manning)
        north_faces = inertial(north_faces, padded[1:-1, :-1], padded[1:-1, 1:], bed_padded[1:-1, :-1], bed_padded[1:-1, 1:], cell_metres, ocean_manning)
        spread = east_faces[1:] - east_faces[:-1] + north_faces[:, 1:] - north_faces[:, :-1]
        water_level = water_level - step_seconds / cell_metres * spread + step_seconds / (cell_metres * cell_metres) * source
        sampled.append(water_level.reshape(-1)[target].reshape(NBLK, MPB))
    mouth_level = jnp.stack(sampled, axis=1).reshape(NBLK, STEPS * MPB)
    return water_depth, water_level, mouth_level
```

```python
import jax
import jax.numpy as jnp
from jax import lax
from jax.experimental import pallas as pl
from jax.experimental.pallas import tpu as pltpu
from jax.sharding import PartitionSpec as P

RB = 128
MPB = 32
STEPS = 12
TX = 32
TY = 128
REACH = 16

gravity = 9.81
step_seconds = 300.0
cell_metres = 3000.0
river_manning = 0.035
ocean_manning = 0.025
depth_floor = 0.05
GT = gravity * step_seconds
POWER = -7.0 / 3.0

F32 = jnp.float32
BF16 = jnp.bfloat16
I32 = jnp.int32
MESH = pl.DeviceIdType.MESH
NT = (((1,), (1,)), ((), ()))

WIDTHS = [STEPS - 1 - k for k in range(STEPS)]
STARTS = [sum(WIDTHS[:k]) for k in range(STEPS)]
VM = pl.BlockSpec(memory_space=pltpu.VMEM)
ROWS, COLS = 56, 256


def struct(*shape, dtype=F32):
    return jax.ShapeDtypeStruct(shape, dtype)


def iota(shape, axis):
    return lax.broadcasted_iota(I32, shape, axis)


def split(value):
    high = value.astype(BF16).astype(F32)
    return high, value - high


def lanes(value, shift):
    shift = shift % value.shape[1]
    return value if shift == 0 else pltpu.roll(value, shift, axis=1)


def friction(unit_flow, face_depth, manning):
    floor = jnp.maximum(face_depth, depth_floor)
    return 1.0 + (GT * manning * manning) * jnp.abs(unit_flow) * jnp.exp(POWER * jnp.log(floor))


def to_dense16(value):
    return jnp.concatenate([value[16 * q : 16 * q + 16] for q in range(4)], axis=1)


def swap_groups(parts):
    lane = iota(parts[0].shape, 1) // 32
    done = []
    for p in range(4):
        total = lanes(parts[0], -32 * p)
        for q in range(1, 4):
            total = jnp.where(lane == q, lanes(parts[q], 32 * (q - p)), total)
        done.append(total)
    return done


def river_kernel(
    depth_ref, flow_ref, bed_ref, width_ref, length_ref, runoff_ref, into_ref, prev_ref, tile_ref, cell_ref,
    sea_ref, seabed_ref, wet_ref, east_ref, north_ref,
    depth_out, send_out, tile_out, slot_out, fields_out, left_out, right_out,
    masks, series,
):
    seabed = seabed_ref[...]
    level = jnp.where(wet_ref[...] == 1, jnp.maximum(sea_ref[...], seabed), seabed)
    fields = [level, seabed, east_ref[...], north_ref[...]]
    lane = iota((TX, TY), 1)
    left = fields[0]
    right = lanes(fields[0], 16)
    for i in range(4):
        fields_out[i] = fields[i]
        if i:
            left = jnp.where(lane // 16 == i, lanes(fields[i], 16 * i), left)
            right = jnp.where(lane // 16 == i, lanes(fields[i], 16 * i + 16), right)
    left_out[...] = left
    right_out[...] = right

    tile = to_dense16(jnp.transpose(tile_ref[:, 0, :]))
    cell = to_dense16(jnp.transpose(cell_ref[...]))
    tile_out[...] = tile
    upper = (iota((128, 256), 0) < iota((128, 256), 1)).astype(F32).astype(BF16)
    tiles_of = iota((128, 128), 0)
    carry = jnp.zeros((128, 128), F32)
    hits, ranks = [], []
    for a in range(16):
        hit = (tiles_of == tile[a : a + 1, :]).astype(F32)
        hits.append(hit.astype(BF16))
        counted = jnp.dot(hits[a], upper, preferred_element_type=F32)
        ranks.append(jnp.sum(hit * (counted[:, :128] + carry), axis=0, keepdims=True))
        carry = carry + counted[:, 128:]
    slot = jnp.concatenate(ranks, axis=0).astype(I32)
    slot_out[...] = slot

    bed, width, into = bed_ref[...], width_ref[...], into_ref[...]
    lane = iota((64, RB), 1)
    inland = lane < RB - MPB
    index = jnp.minimum(into, RB - 1)
    below_bed = jnp.where(inland, jnp.take_along_axis(bed, index, axis=1, mode="promise_in_bounds"), bed)
    previous = jnp.concatenate([jnp.zeros((64, RB - MPB), F32), jnp.transpose(prev_ref[...])], axis=1)
    for offset in range(1, REACH + 1):
        masks[offset - 1] = (pltpu.roll(into, offset, axis=1) == lane).astype(F32)
    face_bed = jnp.maximum(bed, below_bed)
    pull = GT / length_ref[...]
    rate = step_seconds / (width * length_ref[...])
    runoff = runoff_ref[...]

    def turn(step, carry):
        depth, flow = carry
        surface = bed + depth
        below = jnp.where(inland, jnp.take_along_axis(surface, index, axis=1, mode="promise_in_bounds"), previous)
        face = jnp.maximum(surface, below) - face_bed
        drive = pull * jnp.maximum(face, 0.0) * (surface - below)
        flow = (flow + drive) / friction(flow, face, river_manning)
        discharge = flow * width
        inflow = runoff - discharge
        for offset in range(1, REACH + 1):
            inflow = inflow + masks[offset - 1] * pltpu.roll(discharge, offset, axis=1)
        series[step] = to_dense16(discharge[:, RB - MPB :])
        return depth + rate * inflow, flow

    depth, _ = lax.fori_loop(0, STEPS, turn, (depth_ref[...], flow_ref[...]))
    depth_out[...] = depth

    cells = cell.astype(F32)
    slots_of = iota((32, 128), 0)
    total = jnp.zeros((128, 512), F32)
    for a in range(16):
        mine = slots_of == slot[a : a + 1, :]
        pieces = []
        for k in range(STEPS + 1):
            row = series[k, a : a + 1, :] if k < STEPS else cells[a : a + 1, :]
            pieces.append(
                jnp.concatenate(
                    [jnp.where(mine, part, 0.0).astype(BF16) for part in split(row)], axis=1
                )
            )
        weights = jnp.concatenate(pieces + [pieces[-1]] * 3, axis=0)
        both = jnp.concatenate([hits[a], hits[a]], axis=1)
        total = total + lax.dot_general(both, weights, NT, preferred_element_type=F32)
    for j in range(4):
        send_out[:, j, :] = total[:, 128 * j : 128 * j + 128]


def source_kernel(recv_ref, src_out, left_out, right_out, row_out, col_out):
    lane = iota((32, 128), 1)
    dense = []
    for j in range(3):
        dense += swap_groups([recv_ref[32 * q : 32 * q + 32, j, :] for q in range(4)])
    cell = recv_ref[0:32, 3, :]
    for q in range(1, 4):
        cell = jnp.where(lane // 32 == q, recv_ref[32 * q : 32 * q + 32, 3, :], cell)
    cell = cell.astype(I32)
    row, col = cell // TY, cell % TY
    row_out[...] = row
    col_out[...] = col
    halves = [split(value) for value in dense]
    rows_of, cols_of = iota((TX, 128), 0), iota((TY, 128), 0)
    total = jnp.zeros((STEPS * TX, TY), F32)
    for a in range(32):
        mine = rows_of == row[a : a + 1, :]
        there = (cols_of == col[a : a + 1, :]).astype(F32).astype(BF16)
        pieces = [
            jnp.concatenate([jnp.where(mine, part[a : a + 1, :], 0.0).astype(BF16) for part in pair], axis=1)
            for pair in halves
        ]
        total = total + lax.dot_general(
            jnp.concatenate(pieces, axis=0), jnp.concatenate([there, there], axis=1), NT, preferred_element_type=F32
        )
    left = right = jnp.zeros((TX, TY), F32)
    for k in range(STEPS):
        now = total[TX * k : TX * k + TX] * (step_seconds / (cell_metres * cell_metres))
        src_out[k] = now
        if WIDTHS[k]:
            here = (lane >= STARTS[k]) & (lane < STARTS[k] + WIDTHS[k])
            left = jnp.where(here, lanes(now, STARTS[k]), left)
            right = jnp.where(here, lanes(now, STARTS[k] - (TY - WIDTHS[k])), right)
    left_out[...] = left
    right_out[...] = right


def stack_rows(own, low, up):
    upper_half = iota((8, own.shape[1]), 0) >= 4
    return jnp.concatenate(
        [own, low[0:8], jnp.where(upper_half, up[0:8], low[8:16]), up[8:16]], axis=0
    )


def ocean_kernel(
    fields_ref, flow_ref, fup_ref, fpr_ref, fpl_ref, fcor_ref,
    src_ref, slow_ref, sup_ref, spr_ref, spl_ref, scor_ref, row_ref, col_ref,
    level_out, reply_out, levels,
):
    river, coast = lax.axis_index("river"), lax.axis_index("coast")
    rivers, coasts = lax.axis_size("river"), lax.axis_size("coast")
    line = iota((ROWS, COLS), 0)
    place = iota((ROWS, COLS), 1)
    line_ok = (line < 32) | ((line < 44) & (river < rivers - 1)) | ((line >= 44) & (river > 0))
    place_ok = (place < 128) | ((place < 192) & (coast < coasts - 1)) | ((place >= 192) & (coast > 0))
    inside = line_ok & place_ok
    half = iota((ROWS, TY), 1) < 64

    from_right = stack_rows(fpr_ref[...], fcor_ref[0], fcor_ref[1])
    from_left = stack_rows(fpl_ref[...], fcor_ref[2], fcor_ref[3])
    state = []
    for i in range(4):
        own = stack_rows(fields_ref[i], flow_ref[i], fup_ref[i])
        side = jnp.where(half, lanes(from_right, -16 * i), lanes(from_left, 112 - 16 * i))
        state.append(jnp.where(inside, jnp.concatenate([own, side], axis=1), 0.0))
    level, bed, east, north = state
    bed_east = jnp.maximum(bed, pltpu.roll(bed, ROWS - 1, axis=0))
    bed_north = jnp.maximum(bed, pltpu.roll(bed, COLS - 1, axis=1))
    next_right = stack_rows(spr_ref[...], scor_ref[0], scor_ref[1])
    next_left = stack_rows(spl_ref[...], scor_ref[2], scor_ref[3])

    def inertial(unit_flow, upper, lower, bed_face):
        face = jnp.maximum(upper, lower) - bed_face
        drive = (GT / cell_metres) * jnp.maximum(face, 0.0) * (upper - lower)
        return (unit_flow + drive) / friction(unit_flow, face, ocean_manning)

    for k in range(STEPS):
        east = inertial(east, level, pltpu.roll(level, ROWS - 1, axis=0), bed_east)
        north = inertial(north, level, pltpu.roll(level, COLS - 1, axis=1), bed_north)
        own = stack_rows(src_ref[k], slow_ref[k], sup_ref[k])
        side = jnp.where(
            half, lanes(next_right, -STARTS[k]), lanes(next_left, TY - WIDTHS[k] - STARTS[k])
        )
        source = jnp.concatenate([own, side], axis=1)
        spread = east - pltpu.roll(east, 1, axis=0) + north - pltpu.roll(north, 1, axis=1)
        level = jnp.where(inside, level - (step_seconds / cell_metres) * spread + source, 0.0)
        levels[TX * k : TX * k + TX, :] = level[0:TX, 0:TY]
    level_out[...] = level[0:TX, 0:TY]

    high, low = split(levels[...])
    table = jnp.concatenate([high.astype(BF16), low.astype(BF16)], axis=1)
    rows_of, cols_of = iota((TX, 128), 0), iota((TY, 128), 0)
    picked = [[] for _ in range(STEPS)]
    for a in range(32):
        there = (cols_of == col_ref[a : a + 1, :]).astype(F32).astype(BF16)
        found = jnp.dot(table, jnp.concatenate([there, there], axis=0), preferred_element_type=F32)
        mine = rows_of == row_ref[a : a + 1, :]
        for k in range(STEPS):
            picked[k].append(jnp.sum(jnp.where(mine, found[TX * k : TX * k + TX], 0.0), axis=0, keepdims=True))
    for j in range(3):
        parts = swap_groups([jnp.concatenate(picked[4 * j + p], axis=0) for p in range(4)])
        for q in range(4):
            reply_out[32 * q : 32 * q + 32, j, :] = parts[q]
    reply_out[:, 3, :] = jnp.zeros((128, 128), F32)


def mouth_kernel(ret_ref, tile_ref, slot_ref, out_ref):
    table = jnp.concatenate([jnp.transpose(ret_ref[:, j, :]) for j in range(3)], axis=0)
    high, low = split(table)
    table = jnp.concatenate([high.astype(BF16), low.astype(BF16)], axis=1)
    tiles_of, slots_of = iota((128, 128), 0), iota((32, 128), 0)
    picked = [[] for _ in range(STEPS)]
    for a in range(16):
        hit = (tiles_of == tile_ref[a : a + 1, :]).astype(F32).astype(BF16)
        found = jnp.dot(table, jnp.concatenate([hit, hit], axis=0), preferred_element_type=F32)
        mine = slots_of == slot_ref[a : a + 1, :]
        for k in range(STEPS):
            picked[k].append(jnp.sum(jnp.where(mine, found[32 * k : 32 * k + 32], 0.0), axis=0, keepdims=True))
    for j in range(3):
        parts = swap_groups([jnp.concatenate(picked[4 * j + p], axis=0) for p in range(4)])
        for q in range(4):
            out_ref[16 * q : 16 * q + 16, 128 * j : 128 * j + 128] = parts[q]


def around():
    river, coast = lax.axis_index("river"), lax.axis_index("coast")
    rivers, coasts = lax.axis_size("river"), lax.axis_size("coast")
    return river, coast, rivers, coasts


def greet(devices):
    barrier = pltpu.get_barrier_semaphore()
    for device in devices:
        pl.semaphore_signal(barrier, inc=1, device_id=device, device_id_type=MESH)
    pl.semaphore_wait(barrier, len(devices))


def ring_devices():
    river, coast, rivers, coasts = around()
    return [((river + d) % rivers, coast) for d in range(1, rivers)] + [
        (river, (coast + d) % coasts) for d in range(1, coasts)
    ]


def beside_devices(corners_only):
    river, coast, rivers, coasts = around()
    devices = [((river + r) % rivers, (coast + c) % coasts) for r in (-1, 1) for c in (-1, 1)]
    if not corners_only:
        devices += [((river + r) % rivers, coast) for r in (-1, 1)]
        devices += [(river, (coast + c) % coasts) for c in (-1, 1)]
    return devices


def remote(src, dst, send, recv, index, device):
    return pltpu.make_async_remote_copy(
        src_ref=src, dst_ref=dst, send_sem=send.at[index], recv_sem=recv.at[index], device_id=device,
        device_id_type=MESH,
    )


def over_river(src, dst, send, recv, local):
    river, coast, rivers, _ = around()
    copies = [
        remote(src.at[(river + d) % rivers], dst.at[river], send, recv, d - 1, ((river + d) % rivers, coast))
        for d in range(1, rivers)
    ]
    return copies, pltpu.make_async_copy(src.at[river], dst.at[river], local)


def over_coast(src, dst, send, recv, local):
    river, coast, _, coasts = around()
    copies = [
        remote(
            src.at[:, (coast + d) % coasts], dst.at[:, coast], send, recv, d - 1, (river, (coast + d) % coasts)
        )
        for d in range(1, coasts)
    ]
    return copies, pltpu.make_async_copy(src.at[:, coast], dst.at[:, coast], local)


def run(copies, local):
    for copy in copies:
        copy.start()
    local.start()
    for copy in copies:
        copy.wait()
    local.wait()


def corner_copies(left, right, corners, send, recv, first):
    river, coast, rivers, coasts = around()
    before, after = (river - 1) % rivers, (river + 1) % rivers
    west, east = (coast - 1) % coasts, (coast + 1) % coasts
    return [
        remote(left.at[0:16], corners.at[0], send, recv, first, (before, west)),
        remote(left.at[16:32], corners.at[1], send, recv, first + 1, (after, west)),
        remote(right.at[0:16], corners.at[2], send, recv, first + 2, (before, east)),
        remote(right.at[16:32], corners.at[3], send, recv, first + 3, (after, east)),
    ]


def side_copies(left, right, from_right, from_left, send, recv, first):
    river, coast, _, coasts = around()
    return [
        remote(left, from_right, send, recv, first, (river, (coast - 1) % coasts)),
        remote(right, from_left, send, recv, first + 1, (river, (coast + 1) % coasts)),
    ]


def row_copies(whole, low, up, send, recv, first):
    river, coast, rivers, _ = around()
    return [
        remote(whole.at[:, 0:16], low, send, recv, first, ((river - 1) % rivers, coast)),
        remote(whole.at[:, 16:32], up, send, recv, first + 1, ((river + 1) % rivers, coast)),
    ]


def outward_kernel(
    send_ref, fields, left, right, recv_out, low, up, from_right, from_left, corners,
    middle, send_r, recv_r, send_c, recv_c, send_h, recv_h, local,
):
    greet(ring_devices() + beside_devices(True))
    copies, own = over_river(send_ref, middle, send_r, recv_r, local.at[0])
    halo = (
        side_copies(left, right, from_right, from_left, send_h, recv_h, 0)
        + row_copies(fields, low, up, send_h, recv_h, 2)
        + corner_copies(left, right, corners, send_h, recv_h, 4)
    )
    run(copies, own)
    for copy in halo:
        copy.start()
    run(*over_coast(middle, recv_out, send_c, recv_c, local.at[1]))
    for copy in halo:
        copy.wait()


def beside_kernel(whole, left, right, low, up, from_right, from_left, corners, send_h, recv_h):
    greet(beside_devices(False))
    halo = (
        side_copies(left, right, from_right, from_left, send_h, recv_h, 0)
        + row_copies(whole, low, up, send_h, recv_h, 2)
        + corner_copies(left, right, corners, send_h, recv_h, 4)
    )
    for copy in halo:
        copy.start()
    for copy in halo:
        copy.wait()


def back_kernel(reply, out, middle, send_r, recv_r, send_c, recv_c, local):
    greet(ring_devices())
    run(*over_coast(reply, middle, send_c, recv_c, local.at[0]))
    run(*over_river(middle, out, send_r, recv_r, local.at[1]))


def call(kernel, outs, scratch=(), remote_id=None):
    params = (
        pltpu.CompilerParams(vmem_limit_bytes=48 * 2**20)
        if remote_id is None
        else pltpu.CompilerParams(vmem_limit_bytes=48 * 2**20, collective_id=remote_id, has_side_effects=True)
    )

    def apply(*args):
        return pl.pallas_call(
            kernel,
            out_shape=outs,
            in_specs=[VM] * len(args),
            out_specs=jax.tree.map(lambda _: VM, outs),
            scratch_shapes=list(scratch),
            compiler_params=params,
        )(*args)

    return apply


def per_device(
    reach_depth, reach_flow, reach_bed, reach_width, reach_length, runoff, flows_into, mouth_prev, mouth_tile,
    mouth_cell, sea_level, sea_bed, wet_mask, flux_east, flux_north,
):
    rivers, coasts = lax.axis_size("river"), lax.axis_size("coast")
    dma = pltpu.SemaphoreType.DMA
    depth_after, send, tile, slot, fields, left, right = call(
        river_kernel,
        (
            struct(64, 128), struct(128, 4, 128), struct(16, 128, dtype=I32), struct(16, 128, dtype=I32),
            struct(4, 32, 128), struct(32, 128), struct(32, 128),
        ),
        (pltpu.VMEM((REACH, 64, 128), F32), pltpu.VMEM((STEPS, 16, 128), F32)),
    )(
        reach_depth, reach_flow, reach_bed, reach_width, reach_length, runoff, flows_into,
        mouth_prev.T, jnp.transpose(mouth_tile, (1, 2, 0)), mouth_cell.T,
        sea_level, sea_bed, wet_mask, flux_east, flux_north,
    )
    halo = (struct(32, 128), struct(32, 128), struct(4, 16, 128))
    recv, *field_halo = call(
        outward_kernel,
        (struct(rivers, coasts, 4, 128), struct(4, 16, 128), struct(4, 16, 128)) + halo,
        (
            pltpu.VMEM((rivers, coasts, 4, 128), F32),
            dma((rivers - 1,)), dma((rivers - 1,)), dma((coasts - 1,)), dma((coasts - 1,)), dma((8,)), dma((8,)),
            dma((2,)),
        ),
        0,
    )(send.reshape(rivers, coasts, 4, 128), fields, left, right)
    sources, left, right, row, col = call(
        source_kernel,
        (
            struct(STEPS, 32, 128), struct(32, 128), struct(32, 128), struct(32, 128, dtype=I32),
            struct(32, 128, dtype=I32),
        ),
    )(recv.reshape(128, 4, 128))
    source_halo = call(
        beside_kernel,
        (struct(STEPS, 16, 128), struct(STEPS, 16, 128)) + halo,
        (dma((8,)), dma((8,))),
        1,
    )(sources, left, right)
    level_after, reply = call(
        ocean_kernel,
        (struct(32, 128), struct(128, 4, 128)),
        (pltpu.VMEM((STEPS * TX, TY), F32),),
    )(fields, *field_halo, sources, *source_halo, row, col)
    returned = call(
        back_kernel,
        struct(rivers, coasts, 4, 128),
        (
            pltpu.VMEM((rivers, coasts, 4, 128), F32),
            dma((rivers - 1,)), dma((rivers - 1,)), dma((coasts - 1,)), dma((coasts - 1,)), dma((2,)),
        ),
        2,
    )(reply.reshape(rivers, coasts, 4, 128))
    mouth_level = call(mouth_kernel, struct(64, 384))(returned.reshape(128, 4, 128), tile, slot)
    return depth_after, level_after, mouth_level


def solution(mesh):
    both = P(("river", "coast"), None)
    grid = P("river", "coast")
    placed = (both,) * 8 + (P(("river", "coast"), None, None), both) + (grid,) * 5
    return jax.shard_map(
        per_device, mesh=mesh, in_specs=placed, out_specs=(both, grid, both), check_vma=False
    )
```
